256 devices in a mesh: expert: 32 (over x, z), tensor: 8 (over y, core).
Axes of the slice: x: 4, y: 4, z: 8, core: 2. Of those that a mesh axis runs over, the one named last changes fastest.
Arguments:
- tokens: bfloat16 [4096, 4096], P('expert', 'tensor'), may hold values from -3 to 3
- norm_gain: float32 [4096], replicated, may hold values from 0.1 to 1.9
- w_gate: bfloat16 [64, 1536, 4096], P('expert', 'tensor'), may hold values from -0.09375 to 0.09375
- w_up: bfloat16 [64, 1536, 4096], P('expert', 'tensor'), may hold values from -0.09375 to 0.09375
- w_down: bfloat16 [64, 1536, 4096], P('expert', 'tensor'), may hold values from -0.15625 to 0.15625
- routes: int32 [4096, 8], P('expert'), may hold values from 0 to 63, all different within a row; in each aligned block of 128 rows (0 to 127, 128 to 255, ...) at most 24 rows name the same one
- shares: int32 [4096, 8], P('expert'), may hold values from 1 to 32
- skipped: int32 [4096], P('expert'), may hold values 0 or 1
Outputs:
- mixed: bfloat16 [4096, 4096], P('expert', 'tensor')
The draws below stay inside these ranges and needn't reach their ends.
Inputs may be any that keep to these rules, and one draw needn't show every extreme that they name: In each aligned block of 128 rows (the rows of one index of expert), no expert is named by more than 24 of the block's routes, and in every draw some block names some expert exactly 24 times; a row names 8 different experts.
All inputs are finite; a program needn't handle non-finite values. No bound on the sum of `skipped` on one device may be relied on, other than what follows from the above.
Results may differ from the reference program's by a relative error of at most 0.012.
Values may be sent and summed in bfloat16 or wider, within the bound.
A program may use at most 128 MiB of HBM per device.

```python
import math
import jax
import jax.numpy as jnp
import numpy as np
from jax import lax

D = 4096
FF = 1536
TOP = 8
TOK_DEV = 128
EXPERTS = 64
TOKENS = 4096
CAP = 24
N_EXPERT = 32
N_TENSOR = 8


def place_ends(result, key, low, largest):
    shape = result.shape
    spot = [jax.random.randint(jax.random.fold_in(key, axis), (), 0, shape[axis]) for axis in range(len(shape))]
    result = result.at[tuple(spot)].set(low)
    longest = shape.index(max(shape))
    spot[longest] = (spot[longest] + 1) % shape[longest]
    return result.at[tuple(spot)].set(largest)


def steps_of(stream_key, dims, pieces, smallest, top_value):
    level = 1.0
    for position, parts in pieces:
        draws = jax.random.uniform(jax.random.fold_in(jax.random.fold_in(stream_key, 6), position), (parts,), jnp.float32, smallest / len(pieces), top_value / len(pieces))
        level = level * jnp.repeat(jnp.exp(draws), dims[position] // parts).reshape((-1,) + (1,) * (len(dims) - 1 - position))
    return level


def deal_out(stream_key, own, number, rows, number_of, top, bound, slope):
    order = jax.random.permutation(stream_key, number_of)
    packed, usual = load_shares(number_of, rows * top, bound, slope, True), load_shares(number_of, rows * top, bound, slope, False)
    places = jnp.arange(number_of)

    def named(sizes, rotation):
        used = int((sizes > 0).sum())
        fixed = max(1, used // 4)
        shifted = fixed + (places - fixed + rotation * (used - fixed)) % max(1, number_of - fixed)
        return jnp.zeros((number_of,), jnp.int32).at[order[jnp.where(places < fixed, places, shifted)]].set(jnp.asarray(sizes, jnp.int32))

    sizes = jnp.where(number % 4 == 0, named(packed, number // 4), named(usual, number - number // 4 - 1))
    mixed = jax.random.permutation(jax.random.fold_in(own, 3), number_of)
    source_of, taker = mixed[0:number_of // 2 * 2:2], mixed[1:number_of // 2 * 2:2]
    margin = jnp.minimum(sizes[source_of] - 1, bound - sizes[taker]) // 2
    margin = jnp.where((source_of == order[0]) | (taker == order[0]) | (sizes[taker] == 0), 0, jnp.maximum(margin, 0))
    shifted = jax.random.randint(jax.random.fold_in(own, 4), (number_of // 2,), 0, 1 << 20) % (margin + 1)
    sizes = sizes.at[source_of].add(-shifted).at[taker].add(shifted)
    members = jnp.searchsorted(jnp.cumsum(sizes), jnp.arange(rows * top), side="right").astype(jnp.int32)
    table = members.reshape(top, rows).T
    table = table[jax.random.permutation(jax.random.fold_in(own, 1), rows)]
    rotation = jax.random.randint(jax.random.fold_in(own, 2), (rows, 1), 0, top)
    return jnp.take_along_axis(table, (jnp.arange(top)[None, :] + rotation) % top, axis=1)


def load_shares(count, total, limit, lean, full):
    portions = [(1 << 20) // math.isqrt(standing ** lean) + 1 for standing in range(1, count + 1)]
    largest = limit if full else min(limit, max(-(-total // count), total * portions[0] // sum(portions)))
    least = 1 if total - largest >= count - 1 else 0
    counts, spare = [largest] + [least] * (count - 1), total - largest - least * (count - 1)
    while spare > 0:
        free = [i for i in range(1, count) if counts[i] < largest] or [i for i in range(1, count) if counts[i] < limit]
        whole, budget = sum([portions[i] for i in free]), spare
        for i in free:
            extra = min(limit - counts[i], max(1, budget * portions[i] // whole), spare)
            counts[i] = counts[i] + extra
            spare = spare - extra
    return np.array(counts)


def gaussian(stream_key, extent, width, limit, cuts=(), kind=jnp.bfloat16):
    entries = width * jax.random.normal(stream_key, extent, jnp.float32)
    if cuts:
        entries = entries * steps_of(stream_key, extent, cuts, -0.22, 0.18)
    return jnp.clip(entries, -limit, limit).astype(kind)


def setup_inputs(seed: int = 0) -> dict:
    arg_keys = jax.random.split(jax.random.key(seed), 9)
    tokens = gaussian(arg_keys[0], (TOKENS, D), 0.5, 3.0, ((0, 32), (1, 8)))
    norm_gain = jnp.clip(1.0 + 0.18 * jax.random.normal(arg_keys[1], (D,), jnp.float32), 0.1, 1.9)
    w_gate = gaussian(arg_keys[2], (EXPERTS, FF, D), D ** -0.5, 0.09375, ((0, 32), (1, 8)))
    w_up = gaussian(arg_keys[3], (EXPERTS, FF, D), D ** -0.5, 0.09375, ((0, 32), (1, 8)))
    w_down = gaussian(arg_keys[4], (EXPERTS, FF, D), FF ** -0.5, 0.15625, ((0, 32), (1, 8)))
    routes_keys = jax.random.split(jax.random.fold_in(arg_keys[5], 1), TOKENS // TOK_DEV)
    routes_turns = jax.random.permutation(jax.random.fold_in(arg_keys[5], 3), TOKENS // TOK_DEV)
    routes = jax.vmap(lambda own, number: deal_out(jax.random.fold_in(arg_keys[5], 2), own, number, TOK_DEV, EXPERTS, TOP, CAP, 2))(routes_keys, routes_turns).reshape((TOKENS, TOP))
    shares = place_ends(jax.random.randint(arg_keys[6], (TOKENS, TOP), 1, 33), jax.random.fold_in(arg_keys[6], 1), 1, 32).astype(jnp.int32)
    skipped = place_ends((jax.random.randint(arg_keys[7], (TOKENS,), 0, 4) < 1).astype(jnp.int32), jax.random.fold_in(arg_keys[7], 1), 0, 1)
    return dict(tokens=tokens, norm_gain=norm_gain, w_gate=w_gate, w_up=w_up, w_down=w_down, routes=routes, shares=shares, skipped=skipped)


def reference(tokens, norm_gain, w_gate, w_up, w_down, routes, shares, skipped):
    values = tokens.astype(jnp.float32)
    meansq = lax.optimization_barrier(jnp.mean(values * values, axis=1, keepdims=True))
    normed = (values * lax.rsqrt(meansq + 1e-06) * norm_gain).astype(jnp.bfloat16)
    weights = shares.astype(jnp.float32)
    coef = weights / lax.optimization_barrier(jnp.sum(weights, axis=1, keepdims=True))
    coef = coef * (1.0 - skipped.astype(jnp.float32))[:, None]
    flat_coef = coef.reshape(-1)
    flat = routes.reshape(-1)
    total = TOKENS * TOP
    most = N_EXPERT * CAP
    slice_width = FF // N_TENSOR
    contract = (((1,), (1,)), ((), ()))

    def one_expert(acc, expert_id):
        found = jnp.nonzero(flat == expert_id, size=most, fill_value=total)[0].astype(jnp.int32)
        valid = found < total
        safe = jnp.where(valid, found, 0).astype(jnp.int32)
        owner = safe // TOP
        rows = normed[owner]
        gate = lax.dot_general(rows, w_gate[expert_id], contract, preferred_element_type=jnp.float32)
        upper = lax.dot_general(rows, w_up[expert_id], contract, preferred_element_type=jnp.float32)
        hidden = (jax.nn.silu(gate) * upper).astype(jnp.bfloat16)
        hsl = hidden.reshape(most, N_TENSOR, slice_width).astype(jnp.float32)
        wsl = w_down[expert_id].reshape(N_TENSOR, slice_width, D).astype(jnp.float32)
        partial_out = jnp.einsum('msf,sfd->msd', hsl, wsl).astype(jnp.bfloat16)
        partial_out = lax.optimization_barrier(partial_out).astype(jnp.float32)
        summed = lax.optimization_barrier(jnp.sum(partial_out, axis=1))
        factor = jnp.where(valid, flat_coef[safe], jnp.zeros((), jnp.float32))
        acc = acc.at[owner].add(summed * factor[:, None])
        return (acc, None)
    start = jnp.zeros((TOKENS, D), jnp.float32)
    moe, _ = lax.scan(one_expert, start, jnp.arange(EXPERTS, dtype=jnp.int32))
    return (values + moe).astype(jnp.bfloat16)
```

```python
import jax
import jax.numpy as jnp
from jax import lax
from jax.sharding import PartitionSpec as P


def slot_tables(routes, coef, inv_rms, all_exp, capacity):
    tok_rows = routes.shape[0]
    hit = routes[:, :, None] == jnp.arange(all_exp, dtype=jnp.int32)[None, None, :]
    named = jnp.any(hit, axis=1)
    weight = jnp.sum(jnp.where(hit, coef[:, :, None], 0.0), axis=1)
    before = jnp.cumsum(named.astype(jnp.int32), axis=0) - 1
    slot = jnp.arange(capacity, dtype=jnp.int32)
    put = named.T[:, None, :] & (before.T[:, None, :] == slot[None, :, None])
    ids = jnp.arange(tok_rows, dtype=jnp.float32)
    token = jnp.sum(jnp.where(put, ids[None, None, :], 0.0), axis=2)
    scale = jnp.sum(jnp.where(put, weight.T[:, None, :], 0.0), axis=2)
    norm = jnp.sum(jnp.where(put, inv_rms[None, None, :], 0.0), axis=2)
    return jnp.stack([token, scale, norm], axis=0)


def body(tokens, norm_gain, w_gate, w_up, w_down, routes, shares, skipped):
    groups = lax.axis_size("expert")
    tparts = lax.axis_size("tensor")
    tok_rows, top_k = routes.shape
    local_exp = w_gate.shape[0]
    all_exp = local_exp * groups
    capacity = tok_rows * top_k * 3 // (2 * all_exp)
    slice_feat = tokens.shape[1]
    full_feat = slice_feat * tparts
    me = lax.axis_index("tensor")

    weights = shares.astype(jnp.float32)
    coef = weights / jnp.sum(weights, axis=1, keepdims=True)
    coef = coef * (1.0 - skipped.astype(jnp.float32))[:, None]

    values = tokens.astype(jnp.float32)
    gain = lax.dynamic_slice(norm_gain, (me * slice_feat,), (slice_feat,))
    scaled = (values * gain[None, :]).astype(jnp.bfloat16)
    sumsq = lax.psum(jnp.sum(values * values, axis=1), "tensor")
    inv_rms = lax.rsqrt(sumsq / full_feat + 1e-06)

    tables = slot_tables(routes, coef, inv_rms, all_exp, capacity)
    tables = tables.reshape(3, groups, local_exp * capacity).transpose(1, 0, 2).reshape(groups, -1)
    tables = lax.all_to_all(tables, "expert", split_axis=0, concat_axis=0, tiled=True)
    tables = tables.reshape(groups, 3, local_exp, capacity)
    rows = groups * capacity
    block = jnp.arange(groups, dtype=jnp.int32)[:, None, None] * tok_rows
    token = (tables[:, 0].astype(jnp.int32) + block).transpose(1, 0, 2).reshape(-1)
    scale = tables[:, 1].transpose(1, 0, 2).reshape(-1)
    norm = tables[:, 2].transpose(1, 0, 2).reshape(local_exp, rows)

    every = lax.all_gather(scaled, "expert", axis=0, tiled=True)
    picked = every[token]
    full = lax.all_gather(picked, "tensor", axis=1, tiled=True).reshape(local_exp, rows, full_feat)
    gate = jnp.einsum("erd,efd->erf", full, w_gate, preferred_element_type=jnp.float32) * norm[:, :, None]
    upper = jnp.einsum("erd,efd->erf", full, w_up, preferred_element_type=jnp.float32) * norm[:, :, None]
    hidden = (jax.nn.silu(gate) * upper).astype(jnp.bfloat16)
    partial_out = jnp.einsum("erf,efd->erd", hidden, w_down, preferred_element_type=jnp.float32)
    rounded = partial_out.astype(jnp.bfloat16).reshape(local_exp * rows, full_feat)
    summed = lax.psum_scatter(rounded, "tensor", scatter_dimension=1, tiled=True)
    weighted = summed.astype(jnp.float32) * scale[:, None]
    spread = jnp.zeros((groups * tok_rows, slice_feat), jnp.float32).at[token].add(weighted)
    moe = lax.psum_scatter(spread.astype(jnp.bfloat16), "expert", scatter_dimension=0, tiled=True)
    return (values + moe.astype(jnp.float32)).astype(jnp.bfloat16)


def solution(mesh):
    return jax.shard_map(
        body,
        mesh=mesh,
        in_specs=(
            P("expert", "tensor"),
            P(),
            P("expert", "tensor", None),
            P("expert", "tensor", None),
            P("expert", "tensor", None),
            P("expert", None),
            P("expert", None),
            P("expert"),
        ),
        out_specs=P("expert", "tensor"),
        check_vma=False,
    )
```

```python
import functools

import jax
import jax.numpy as jnp
from jax import lax
from jax.experimental import pallas as pl
from jax.experimental.pallas import tpu as pltpu
from jax.sharding import PartitionSpec as P

MESH = pl.DeviceIdType.MESH
LINE_Z = 8
CORES = 2
F32 = jnp.float32
BF16 = jnp.bfloat16


def kernel(
    nx, nz, ny, cap, full_feat,
    tokens_ref, gain_ref, routes_ref, shares_ref, skipped_ref, wg_hbm, wu_hbm, wd_hbm,
    out_ref,
    wg, wu, wd, sums, pick, share, normed, outgoing, rows_in, acc, part, pair_in, line_in, done, back, total,
    w_sem, sum_send, sum_recv, disp_send, disp_recv, ag_send, ag_recv,
    pair_send, pair_recv, line_send, line_recv, ret_send, ret_recv,
):
    ne = nx * nz
    nt = ny * CORES
    tok = tokens_ref.shape[0]
    feat = tokens_ref.shape[1]
    two = wg.shape[0]
    blk = 2 * cap
    chunk = nx * blk
    e = lax.axis_index("expert")
    t = lax.axis_index("tensor")
    x, z = e // nz, e % nz
    y, c = t // CORES, t % CORES
    sib = y * CORES + (1 - c)

    def shift(p):
        j, dx = p // nx, p % nx
        half, odd = (j + 1) // 2, j % 2
        return dx, odd * half + (1 - odd) * ((nz - half) % nz)

    def expert_peer(p, sign):
        dx, dz = shift(p)
        return ((x + sign * dx + nx) % nx) * nz + (z + sign * dz + nz) % nz

    def tensor_peer(dy, core):
        return ((y + dy + ny) % ny) * CORES + core

    barrier = pltpu.get_barrier_semaphore()

    def greet_e(p, _):
        pl.semaphore_signal(barrier, inc=1, device_id=(expert_peer(p, 1), t), device_id_type=MESH)
        return 0

    def greet_t(k, _):
        pl.semaphore_signal(barrier, inc=1, device_id=(e, (t + k) % nt), device_id_type=MESH)
        return 0

    weights = [
        pltpu.make_async_copy(hbm, vmem, w_sem.at[i])
        for i, (hbm, vmem) in enumerate(((wg_hbm, wg), (wu_hbm, wu), (wd_hbm, wd)))
    ]
    for copy in weights:
        copy.start()
    lax.fori_loop(1, ne, greet_e, 0)
    lax.fori_loop(1, nt, greet_t, 0)

    eye = (
        lax.broadcasted_iota(jnp.int32, (tok, tok), 0) == lax.broadcasted_iota(jnp.int32, (tok, tok), 1)
    ).astype(F32)
    values = tokens_ref[...].astype(F32)
    column = jnp.sum(values * values, axis=1, keepdims=True)
    row = jnp.sum(eye * column, axis=0, keepdims=True)
    sums[0] = jnp.broadcast_to(row, (8, tok))
    pl.semaphore_wait(barrier, ne - 1 + nt - 1)

    def sum_copy(k):
        return pltpu.make_async_remote_copy(
            sums.at[0], sums.at[k], sum_send.at[k], sum_recv.at[k],
            device_id=(e, (t + k) % nt), device_id_type=MESH,
        )

    def start_sum(k, _):
        sum_copy(k).start()
        return 0

    lax.fori_loop(1, nt, start_sum, 0)

    def turned(ref):
        return lax.dot_general(
            ref[...].astype(F32).astype(BF16), eye.astype(BF16), (((0,), (0,)), ((), ())),
            preferred_element_type=F32,
        )

    routes_t, shares_t = turned(routes_ref), turned(shares_ref)
    ids = lax.broadcasted_iota(jnp.int32, (2 * ne, tok), 0)
    expert_id = (2 * expert_peer(ids // 2, 1) + ids % 2).astype(F32)
    named = jnp.zeros((2 * ne, tok), F32)
    weight = jnp.zeros((2 * ne, tok), F32)
    for k in range(routes_t.shape[0]):
        hit = (expert_id == routes_t[k : k + 1, :]).astype(F32)
        named = named + hit
        weight = weight + hit * shares_t[k : k + 1, :]
    earlier = (
        lax.broadcasted_iota(jnp.int32, (tok, tok), 0) < lax.broadcasted_iota(jnp.int32, (tok, tok), 1)
    ).astype(F32).astype(BF16)
    slot = lax.dot_general(
        named.astype(BF16), earlier, (((1,), (0,)), ((), ())), preferred_element_type=F32
    )
    slot = jnp.where(named > 0.0, slot, -1.0)
    place = lax.broadcasted_iota(jnp.int32, (cap, tok), 0).astype(F32)
    for r in range(2 * ne):
        match = (slot[r : r + 1, :] == place).astype(F32)
        pick[r * cap : (r + 1) * cap, :] = match
        share[r * cap : (r + 1) * cap, :] = match * weight[r : r + 1, :]

    def wait_sum(k, square):
        sum_copy(k).wait()
        return square + sums[k, 0:1, :]

    square = lax.fori_loop(1, nt, wait_sum, row)
    factor = lax.rsqrt(square * (1.0 / full_feat) + 1e-06)
    factor = jnp.sum(eye * factor, axis=1, keepdims=True)
    gain = gain_ref[pl.ds(t, 1), :]
    normed[...] = (values * factor * gain).astype(BF16)

    def dispatch(p):
        rows = pl.ds(p * blk, blk)
        return pltpu.make_async_remote_copy(
            outgoing.at[rows], rows_in.at[t, rows], disp_send.at[p], disp_recv.at[p],
            device_id=(expert_peer(p, 1), t), device_id_type=MESH,
        )

    def select(j, _):
        rows = pl.ds(j * chunk, chunk)
        outgoing[rows, :] = jnp.dot(
            pick[rows, :].astype(BF16), normed[...], preferred_element_type=F32
        ).astype(BF16)

        def start(i, _):
            p = j * nx + i

            @pl.when(p > 0)
            def _():
                dispatch(p).start()

            return 0

        return lax.fori_loop(0, nx, start, 0)

    lax.fori_loop(0, nz, select, 0)
    rows_in[t, 0:blk, :] = outgoing[0:blk, :]

    def gather(j, k):
        rows = pl.ds(j * chunk, chunk)
        if k == 0:
            source, target = t, sib
        elif k < ny:
            source, target = t, tensor_peer(k, c)
        else:
            source, target = tensor_peer(-(k - ny + 1), c), sib
        return pltpu.make_async_remote_copy(
            rows_in.at[source, rows], rows_in.at[source, rows], ag_send.at[j, k], ag_recv.at[j, k],
            device_id=(e, target), device_id_type=MESH,
        )

    def gathered(j, k):
        rows = pl.ds(j * chunk, chunk)
        if k == 0:
            source = sib
        elif k < ny:
            source = tensor_peer(-k, c)
        else:
            source = tensor_peer(-(k - ny + 1), 1 - c)
        return pltpu.make_async_remote_copy(
            rows_in.at[source, rows], rows_in.at[source, rows], ag_send.at[j, k], ag_recv.at[j, k],
            device_id=(e, sib), device_id_type=MESH,
        )

    def pair(j):
        rows = pl.ds(j * chunk, chunk)
        return pltpu.make_async_remote_copy(
            part.at[1 - c, :, rows], pair_in.at[:, rows], pair_send.at[j], pair_recv.at[j],
            device_id=(e, sib), device_id_type=MESH,
        )

    def line(j, dy):
        rows = pl.ds(j * chunk, chunk)
        return pltpu.make_async_remote_copy(
            part.at[c, (y + dy) % ny, rows], line_in.at[dy - 1, rows],
            line_send.at[j, dy - 1], line_recv.at[j, dy - 1],
            device_id=(e, tensor_peer(dy, c)), device_id_type=MESH,
        )

    def give_back(p):
        rows = pl.ds(p * blk, blk)
        return pltpu.make_async_remote_copy(
            done.at[rows], back.at[rows], ret_send.at[p], ret_recv.at[p],
            device_id=(expert_peer(p, -1), t), device_id_type=MESH,
        )

    def stage_gather(j):
        def arrived(i, _):
            p = j * nx + i

            @pl.when(p > 0)
            def _():
                dispatch(p).wait_recv()

            return 0

        lax.fori_loop(0, nx, arrived, 0)
        for k in range(ny):
            gather(j, (k + 1) % ny).start()

    def stage_forward(j):
        for k in range(1, ny):
            gathered(j, k).wait_recv()
            gather(j, ny - 1 + k).start()

    def stage_expert(j):
        @pl.when(j == 0)
        def _():
            for copy in weights:
                copy.wait()

        gathered(j, 0).wait_recv()
        for k in range(ny, 2 * ny - 1):
            gathered(j, k).wait_recv()
        rows = pl.ds(j * chunk, chunk)
        acc[...] = jnp.zeros_like(acc)

        def up(s, _):
            cols = pl.ds(pl.multiple_of(s * feat, feat), feat)
            block = rows_in[s, rows, :]
            nt_dims = (((1,), (1,)), ((), ()))
            acc[0] += lax.dot_general(block, wg[:, cols], nt_dims, preferred_element_type=F32)
            acc[1] += lax.dot_general(block, wu[:, cols], nt_dims, preferred_element_type=F32)
            return 0

        lax.fori_loop(0, nt, up, 0)
        first_row = lax.broadcasted_iota(jnp.int32, (chunk, two), 0) % blk < cap
        first_col = lax.broadcasted_iota(jnp.int32, (chunk, two), 1) < two // 2
        gate = acc[0]
        hidden = gate * jax.nn.sigmoid(gate) * acc[1]
        hidden = jnp.where(first_row == first_col, hidden, 0.0).astype(BF16)

        def down(s, _):
            cols = pl.ds(pl.multiple_of(s * feat, feat), feat)
            part[s % CORES, s // CORES, rows, :] = jnp.dot(
                hidden, wd[:, cols], preferred_element_type=F32
            ).astype(BF16)
            return 0

        lax.fori_loop(0, nt, down, 0)
        pair(j).start()

    def stage_pair(j):
        rows = pl.ds(j * chunk, chunk)
        pair(j).wait_recv()
        for dy in range(1, ny):
            to = (y + dy) % ny
            part[c, to, rows, :] = (
                part[c, to, rows, :].astype(F32) + pair_in[to, rows, :].astype(F32)
            ).astype(BF16)
            line(j, dy).start()

    def stage_line(j):
        rows = pl.ds(j * chunk, chunk)
        result = part[c, y, rows, :].astype(F32) + pair_in[y, rows, :].astype(F32)
        for dy in range(1, ny):
            line(j, dy).wait_recv()
            result = result + line_in[dy - 1, rows, :].astype(F32)
        done[rows, :] = result.astype(BF16)

        def start(i, _):
            p = j * nx + i

            @pl.when(p > 0)
            def _():
                give_back(p).start()

            return 0

        lax.fori_loop(0, nx, start, 0)

        @pl.when(j == 0)
        def _():
            back[0:blk, :] = done[0:blk, :]

    def stage_mix(j):
        rows = pl.ds(j * chunk, chunk)

        def arrived(i, _):
            p = j * nx + i

            @pl.when(p > 0)
            def _():
                give_back(p).wait_recv()

            return 0

        lax.fori_loop(0, nx, arrived, 0)
        total[...] += lax.dot_general(
            share[rows, :].astype(BF16), back[rows, :], (((0,), (0,)), ((), ())),
            preferred_element_type=F32,
        )

    total[...] = jnp.zeros_like(total)
    stages = (
        (0, stage_gather), (1, stage_forward), (2, stage_expert), (3, stage_pair), (5, stage_line), (7, stage_mix),
    )

    def step(i, _):
        for lag, stage in stages:
            @pl.when((i >= lag) & (i < nz + lag))
            def _(lag=lag, stage=stage):
                stage(i - lag)

        return 0

    lax.fori_loop(0, nz + stages[-1][0], step, 0)

    lax.fori_loop(1, ne, lambda p, _: (dispatch(p).wait_send(), give_back(p).wait_send(), 0)[2], 0)

    def drain(j, _):
        for k in range(2 * ny - 1):
            gather(j, k).wait_send()
        pair(j).wait_send()
        for dy in range(1, ny):
            line(j, dy).wait_send()
        return 0

    lax.fori_loop(0, nz, drain, 0)

    of_shares = jnp.sum(shares_ref[...].astype(F32), axis=1, keepdims=True)
    skip = jnp.sum(eye * skipped_ref[...].astype(F32), axis=1, keepdims=True)
    out_ref[...] = (values + total[...] / of_shares * (1.0 - skip)).astype(BF16)


def body(tokens, norm_gain, w_gate, w_up, w_down, routes, shares, skipped):
    ne = lax.axis_size("expert")
    nt = lax.axis_size("tensor")
    nz = LINE_Z
    nx = ne // nz
    ny = nt // CORES
    tok, feat = tokens.shape
    top = routes.shape[1]
    local, ff, full = w_gate.shape
    cap = tok * top * 3 // (2 * local * ne)
    rows = ne * local * cap
    chunk = nx * local * cap
    flat = [w.reshape(local * ff, full) for w in (w_gate, w_up, w_down)]
    vmem = pl.BlockSpec(memory_space=pltpu.VMEM)
    hbm = pl.BlockSpec(memory_space=pl.ANY)
    dma = pltpu.SemaphoreType.DMA
    return pl.pallas_call(
        functools.partial(kernel, nx, nz, ny, cap, full),
        out_shape=jax.ShapeDtypeStruct((tok, feat), BF16),
        in_specs=[vmem] * 5 + [hbm] * 3,
        out_specs=vmem,
        scratch_shapes=[
            pltpu.VMEM((local * ff, full), BF16),
            pltpu.VMEM((local * ff, full), BF16),
            pltpu.VMEM((local * ff, full), BF16),
            pltpu.VMEM((nt, 8, tok), F32),
            pltpu.VMEM((rows, tok), F32),
            pltpu.VMEM((rows, tok), F32),
            pltpu.VMEM((tok, feat), BF16),
            pltpu.VMEM((rows, feat), BF16),
            pltpu.VMEM((nt, rows, feat), BF16),
            pltpu.VMEM((2, chunk, local * ff), F32),
            pltpu.VMEM((CORES, ny, rows, feat), BF16),
            pltpu.VMEM((ny, rows, feat), BF16),
            pltpu.VMEM((ny - 1, rows, feat), BF16),
            pltpu.VMEM((rows, feat), BF16),
            pltpu.VMEM((rows, feat), BF16),
            pltpu.VMEM((tok, feat), F32),
            dma((3,)),
            dma((nt,)),
            dma((nt,)),
            dma((ne,)),
            dma((ne,)),
            dma((nz, 2 * ny - 1)),
            dma((nz, 2 * ny - 1)),
            dma((nz,)),
            dma((nz,)),
            dma((nz, ny - 1)),
            dma((nz, ny - 1)),
            dma((ne,)),
            dma((ne,)),
        ],
        compiler_params=pltpu.CompilerParams(
            collective_id=0, has_side_effects=True, vmem_limit_bytes=60 * 2**20
        ),
    )(tokens, norm_gain.reshape(nt, feat), routes, shares, skipped.reshape(1, tok), *flat)


def solution(mesh):
    return jax.shard_map(
        body,
        mesh=mesh,
        in_specs=(
            P("expert", "tensor"),
            P(),
            P("expert", "tensor", None),
            P("expert", "tensor", None),
            P("expert", "tensor", None),
            P("expert", None),
            P("expert", None),
            P("expert"),
        ),
        out_specs=P("expert", "tensor"),
        check_vma=False,
    )
```

```python
import functools

import jax
import jax.numpy as jnp
from jax import lax
from jax.experimental import pallas as pl
from jax.experimental.pallas import tpu as pltpu
from jax.sharding import PartitionSpec as P

MESH = pl.DeviceIdType.MESH
LINE_Z = 8
CORES = 2
F32 = jnp.float32
BF16 = jnp.bfloat16


def kernel(
    nx, nz, ny, cap, full_feat,
    tokens_ref, gain_ref, routes_ref, shares_ref, skipped_ref, wg_hbm, wu_hbm, wd_hbm,
    out_ref,
    wg, wu, wd, sums, pick, share, normed, outgoing, rows_in, acc, part, pair_in, hop_in, line_in, done, back, total,
    w_sem, sum_send, sum_recv, disp_send, disp_recv, ag_send, ag_recv, fw_send, fw_recv,
    pair_send, pair_recv, hop_send, hop_recv, line_send, line_recv, ret_send, ret_recv,
):
    ne = nx * nz
    nt = ny * CORES
    tok = tokens_ref.shape[0]
    feat = tokens_ref.shape[1]
    two = wg.shape[0]
    blk = 2 * cap
    chunk = nx * blk
    e = lax.axis_index("expert")
    t = lax.axis_index("tensor")
    x, z = e // nz, e % nz
    y, c = t // CORES, t % CORES
    sib = y * CORES + (1 - c)

    order = [1, nz - 1, 2, nz - 2, 4, 3, nz - 3, 0] if nz == 8 else list(range(1, nz)) + [0]
    local = order.index(0)

    def wrap(v, n):
        v = jnp.where(v >= n, v - n, v)
        return jnp.where(v < 0, v + n, v)

    def offset(j):
        if isinstance(j, int):
            return order[j]
        return sum(jnp.where(j == k, dz, 0) for k, dz in enumerate(order))

    def expert_peer(j, dx, sign):
        return wrap(x + sign * dx, nx) * nz + wrap(z + sign * offset(j), nz)

    def tensor_peer(dy, core):
        return wrap(y + dy, ny) * CORES + core

    barrier = pltpu.get_barrier_semaphore()

    weights = [
        pltpu.make_async_copy(hbm, vmem, w_sem.at[i])
        for i, (hbm, vmem) in enumerate(((wg_hbm, wg), (wu_hbm, wu), (wd_hbm, wd)))
    ]
    for copy in weights:
        copy.start()
    for k in range(1, nt):
        pl.semaphore_signal(barrier, inc=1, device_id=(e, wrap(t + k, nt)), device_id_type=MESH)
    for j in range(nz):
        for dx in range(nx):
            if j != local or dx:
                pl.semaphore_signal(barrier, inc=1, device_id=(expert_peer(j, dx, 1), t), device_id_type=MESH)

    eye = (
        lax.broadcasted_iota(jnp.int32, (tok, tok), 0) == lax.broadcasted_iota(jnp.int32, (tok, tok), 1)
    ).astype(F32)
    values = tokens_ref[...].astype(F32)
    column = jnp.sum(values * values, axis=1, keepdims=True)
    row = jnp.sum(eye * column, axis=0, keepdims=True)
    sums[0] = jnp.broadcast_to(row, (8, tok))
    pl.semaphore_wait(barrier, ne - 1 + nt - 1)

    def sum_copy(k):
        return pltpu.make_async_remote_copy(
            sums.at[0], sums.at[k], sum_send.at[k], sum_recv.at[k],
            device_id=(e, wrap(t + k, nt)), device_id_type=MESH,
        )

    for k in range(1, nt):
        sum_copy(k).start()

    routes_t, shares_t = routes_ref[...].astype(F32), shares_ref[...].astype(F32)
    ids = lax.broadcasted_iota(jnp.int32, (2 * ne, tok), 0)
    expert_id = (2 * expert_peer(ids // (2 * nx), ids // 2 % nx, 1) + ids % 2).astype(F32)
    named = jnp.zeros((2 * ne, tok), F32)
    weight = jnp.zeros((2 * ne, tok), F32)
    for k in range(routes_t.shape[0]):
        hit = (expert_id == routes_t[k : k + 1, :]).astype(F32)
        named = named + hit
        weight = weight + hit * shares_t[k : k + 1, :]
    earlier = (
        lax.broadcasted_iota(jnp.int32, (tok, tok), 0) < lax.broadcasted_iota(jnp.int32, (tok, tok), 1)
    ).astype(F32).astype(BF16)
    slot = lax.dot_general(
        named.astype(BF16), earlier, (((1,), (0,)), ((), ())), preferred_element_type=F32
    )
    slot = jnp.where(named > 0.0, slot, -1.0)
    place = lax.broadcasted_iota(jnp.int32, (cap, tok), 0).astype(F32)
    for r in range(2 * ne):
        match = (slot[r : r + 1, :] == place).astype(F32)
        pick[r * cap : (r + 1) * cap, :] = match
        share[r * cap : (r + 1) * cap, :] = match * weight[r : r + 1, :]

    square = row
    for k in range(1, nt):
        sum_copy(k).wait()
        square = square + sums[k, 0:1, :]
    factor = lax.rsqrt(square * (1.0 / full_feat) + 1e-06)
    factor = jnp.sum(eye * factor, axis=1, keepdims=True)
    lanes = gain_ref.shape[1]
    for q in range(feat // lanes):
        cols = slice(q * lanes, (q + 1) * lanes)
        gain = gain_ref[pl.ds(t * (feat // lanes) + q, 1), :]
        normed[:, cols] = (values[:, cols] * factor * gain).astype(BF16)

    def block(j, dx):
        return pl.ds(j * chunk + dx * blk, blk)

    def dispatch(j, dx):
        return pltpu.make_async_remote_copy(
            outgoing.at[block(j, dx)], rows_in.at[t, block(j, dx)], disp_send.at[j, dx], disp_recv.at[j, dx],
            device_id=(expert_peer(j, dx, 1), t), device_id_type=MESH,
        )

    def give_back(j, dx):
        return pltpu.make_async_remote_copy(
            done.at[block(j, dx)], back.at[block(j, dx)], ret_send.at[j, dx], ret_recv.at[j, dx],
            device_id=(expert_peer(j, dx, -1), t), device_id_type=MESH,
        )

    def each(j, act):
        pl.when(j != local)(lambda: act(0))
        for dx in range(1, nx):
            act(dx)

    def stage_send(j):
        rows = whole(j)
        outgoing[rows, :] = jnp.dot(
            pick[rows, :].astype(BF16), normed[...], preferred_element_type=F32
        ).astype(BF16)
        each(j, lambda dx: dispatch(j, dx).start())

        @pl.when(j == local)
        def _():
            rows_in[t, block(j, 0), :] = outgoing[block(j, 0), :]

    up, down, far = tensor_peer(1, c), tensor_peer(-1, c), tensor_peer(2, c)
    half = chunk // 2

    def along(source, rows, send, recv, target):
        return pltpu.make_async_remote_copy(
            rows_in.at[source, rows], rows_in.at[source, rows], send, recv,
            device_id=(e, target), device_id_type=MESH,
        )

    def whole(j):
        return pl.ds(j * chunk, chunk)

    def piece(j, h):
        return pl.ds(j * chunk + h * half, half)

    def own_up(j, source):
        return along(source, whole(j), ag_send.at[j, 0], ag_recv.at[j, 0], up)

    def own_down(j, source):
        return along(source, whole(j), ag_send.at[j, 1], ag_recv.at[j, 1], down)

    def on_up(j, source):
        return along(source, piece(j, 0), ag_send.at[j, 2], ag_recv.at[j, 2], up)

    def on_down(j, source):
        return along(source, piece(j, 1), ag_send.at[j, 3], ag_recv.at[j, 3], down)

    def across(j, k, source):
        return along(source, whole(j), fw_send.at[j, k], fw_recv.at[j, k], sib)

    def pair(j):
        rows = pl.ds(j * chunk, chunk)
        return pltpu.make_async_remote_copy(
            part.at[1 - c, :, rows], pair_in.at[:, rows], pair_send.at[j], pair_recv.at[j],
            device_id=(e, sib), device_id_type=MESH,
        )

    def hop(j, h):
        return pltpu.make_async_remote_copy(
            part.at[c, (y + 2) % ny, piece(j, h)], hop_in.at[h, pl.ds(j * half, half)],
            hop_send.at[j, h], hop_recv.at[j, h],
            device_id=(e, down if h else up), device_id_type=MESH,
        )

    def line(j, h):
        return pltpu.make_async_remote_copy(
            part.at[c, (y + (ny - 1 if h else 1)) % ny, whole(j)], line_in.at[h, whole(j)],
            line_send.at[j, h], line_recv.at[j, h],
            device_id=(e, down if h else up), device_id_type=MESH,
        )

    def stage_gather(j):
        each(j, lambda dx: dispatch(j, dx).wait_recv())
        own_up(j, t).start()
        own_down(j, t).start()
        across(j, 0, t).start()

    def stage_forward(j):
        own_up(j, down).wait_recv()
        on_up(j, down).start()
        across(j, 1, down).start()
        own_down(j, up).wait_recv()
        on_down(j, up).start()
        across(j, 2, up).start()

    def stage_far(j):
        on_up(j, far).wait_recv()
        on_down(j, far).wait_recv()
        across(j, 3, far).start()

    def stage_expert(j):
        @pl.when(j == 0)
        def _():
            for copy in weights:
                copy.wait()

        for k, dy in enumerate((0, -1, 1, 2)):
            across(j, k, tensor_peer(dy, 1 - c)).wait_recv()
        rows = whole(j)
        acc[...] = jnp.zeros_like(acc)

        def widen(s, _):
            cols = pl.ds(pl.multiple_of(s * feat, feat), feat)
            lhs = rows_in[s, rows, :]
            nt_dims = (((1,), (1,)), ((), ()))
            acc[0] += lax.dot_general(lhs, wg[:, cols], nt_dims, preferred_element_type=F32)
            acc[1] += lax.dot_general(lhs, wu[:, cols], nt_dims, preferred_element_type=F32)
            return 0

        lax.fori_loop(0, nt, widen, 0)
        first_row = lax.broadcasted_iota(jnp.int32, (chunk, two), 0) % blk < cap
        first_col = lax.broadcasted_iota(jnp.int32, (chunk, two), 1) < two // 2
        gate = acc[0]
        hidden = gate * jax.nn.sigmoid(gate) * acc[1]
        hidden = jnp.where(first_row == first_col, hidden, 0.0).astype(BF16)

        def narrow(s, _):
            cols = pl.ds(pl.multiple_of(s * feat, feat), feat)
            part[s % CORES, s // CORES, rows, :] = jnp.dot(
                hidden, wd[:, cols], preferred_element_type=F32
            ).astype(BF16)
            return 0

        lax.fori_loop(0, nt, narrow, 0)
        pair(j).start()

    def stage_pair(j):
        rows = whole(j)
        pair(j).wait_recv()
        for dy in (2, 1, ny - 1):
            to = (y + dy) % ny
            part[c, to, rows, :] = (
                part[c, to, rows, :].astype(F32) + pair_in[to, rows, :].astype(F32)
            ).astype(BF16)
            if dy == 2:
                hop(j, 0).start()
                hop(j, 1).start()

    def stage_hop(j):
        for h in (0, 1):
            hop(j, h).wait_recv()
            to = (y + (ny - 1 if h else 1)) % ny
            rows = piece(j, h)
            part[c, to, rows, :] = (
                part[c, to, rows, :].astype(F32) + hop_in[h, pl.ds(j * half, half), :].astype(F32)
            ).astype(BF16)
            line(j, h).start()

    def stage_line(j):
        rows = whole(j)
        result = part[c, y, rows, :].astype(F32) + pair_in[y, rows, :].astype(F32)
        for h in (0, 1):
            line(j, h).wait_recv()
            result = result + line_in[h, rows, :].astype(F32)
        done[rows, :] = result.astype(BF16)

        each(j, lambda dx: give_back(j, dx).start())

        @pl.when(j == local)
        def _():
            back[block(j, 0), :] = done[block(j, 0), :]

    def stage_mix(j):
        rows = pl.ds(j * chunk, chunk)

        each(j, lambda dx: give_back(j, dx).wait_recv())
        total[...] += lax.dot_general(
            share[rows, :].astype(BF16), back[rows, :], (((0,), (0,)), ((), ())),
            preferred_element_type=F32,
        )

    total[...] = jnp.zeros_like(total)
    stages = (
        (0, stage_send), (2, stage_gather), (3, stage_forward), (4, stage_far), (5, stage_expert),
        (6, stage_pair), (7, stage_hop), (8, stage_line), (9, stage_mix),
    )

    def step(i, _):
        for lag, stage in stages:
            @pl.when((i >= lag) & (i < nz + lag))
            def _(lag=lag, stage=stage):
                stage(i - lag)

        return 0

    lax.fori_loop(0, nz + stages[-1][0], step, 0)

    def drain(j, _):
        each(j, lambda dx: (dispatch(j, dx).wait_send(), give_back(j, dx).wait_send())[0])
        own_up(j, t).wait_send()
        own_down(j, t).wait_send()
        on_up(j, down).wait_send()
        on_down(j, up).wait_send()
        for k, dy in enumerate((0, -1, 1, 2)):
            across(j, k, tensor_peer(dy, c)).wait_send()
        pair(j).wait_send()
        for h in (0, 1):
            hop(j, h).wait_send()
            line(j, h).wait_send()
        return 0

    lax.fori_loop(0, nz, drain, 0)

    keep = (1.0 - skipped_ref[...].astype(F32)) / jnp.sum(shares_ref[...].astype(F32), axis=0, keepdims=True)
    keep = jnp.sum(eye * keep, axis=1, keepdims=True)
    out_ref[...] = (tokens_ref[...].astype(F32) + total[...] * keep).astype(BF16)


def body(tokens, norm_gain, w_gate, w_up, w_down, routes, shares, skipped):
    ne = lax.axis_size("expert")
    nt = lax.axis_size("tensor")
    nz = LINE_Z
    nx = ne // nz
    ny = nt // CORES
    tok, feat = tokens.shape
    top = routes.shape[1]
    local, ff, full = w_gate.shape
    cap = tok * top * 3 // (2 * local * ne)
    rows = ne * local * cap
    chunk = nx * local * cap
    flat = [w.reshape(local * ff, full) for w in (w_gate, w_up, w_down)]
    vmem = pl.BlockSpec(memory_space=pltpu.VMEM)
    hbm = pl.BlockSpec(memory_space=pl.ANY)
    dma = pltpu.SemaphoreType.DMA
    return pl.pallas_call(
        functools.partial(kernel, nx, nz, ny, cap, full),
        out_shape=jax.ShapeDtypeStruct((tok, feat), BF16),
        in_specs=[vmem] * 5 + [hbm] * 3,
        out_specs=vmem,
        scratch_shapes=[
            pltpu.VMEM((local * ff, full), BF16),
            pltpu.VMEM((local * ff, full), BF16),
            pltpu.VMEM((local * ff, full), BF16),
            pltpu.VMEM((nt, 8, tok), F32),
            pltpu.VMEM((rows, tok), F32),
            pltpu.VMEM((rows, tok), F32),
            pltpu.VMEM((tok, feat), BF16),
            pltpu.VMEM((rows, feat), BF16),
            pltpu.VMEM((nt, rows, feat), BF16),
            pltpu.VMEM((2, chunk, local * ff), F32),
            pltpu.VMEM((CORES, ny, rows, feat), BF16),
            pltpu.VMEM((ny, rows, feat), BF16),
            pltpu.VMEM((2, rows // 2, feat), BF16),
            pltpu.VMEM((2, rows, feat), BF16),
            pltpu.VMEM((rows, feat), BF16),
            pltpu.VMEM((rows, feat), BF16),
            pltpu.VMEM((tok, feat), F32),
            dma((3,)),
            dma((nt,)),
            dma((nt,)),
            dma((nz, nx)),
            dma((nz, nx)),
            dma((nz, 4)),
            dma((nz, 4)),
            dma((nz, 4)),
            dma((nz, 4)),
            dma((nz,)),
            dma((nz,)),
            dma((nz, 2)),
            dma((nz, 2)),
            dma((nz, 2)),
            dma((nz, 2)),
            dma((nz, nx)),
            dma((nz, nx)),
        ],
        compiler_params=pltpu.CompilerParams(
            collective_id=0, has_side_effects=True, vmem_limit_bytes=60 * 2**20
        ),
    )(tokens, norm_gain.reshape(-1, 128), routes.T, shares.T, skipped.reshape(1, tok), *flat)


def solution(mesh):
    return jax.shard_map(
        body,
        mesh=mesh,
        in_specs=(
            P("expert", "tensor"),
            P(),
            P("expert", "tensor", None),
            P("expert", "tensor", None),
            P("expert", "tensor", None),
            P("expert", None),
            P("expert", None),
            P("expert"),
        ),
        out_specs=P("expert", "tensor"),
        check_vma=False,
    )
```

```python
import functools

import jax
import jax.numpy as jnp
from jax import lax
from jax.experimental import pallas as pl
from jax.experimental.pallas import tpu as pltpu
from jax.sharding import PartitionSpec as P

MESH = pl.DeviceIdType.MESH
LINE_Z = 8
CORES = 2
F32 = jnp.float32
BF16 = jnp.bfloat16


def kernel(
    nx, nz, ny, cap, full_feat,
    tokens_ref, gain_ref, routes_ref, shares_ref, skipped_ref, wg_hbm, wu_hbm, wd_hbm,
    out_ref,
    wg, wu, wd, sums, slots, slot_share, pick, share, normed, outgoing, wide_out, rows_in, acc, part, pair_in, hop_in, line_in, done, back, wide_back, total, wide_total, red_out, red_in,
    w_sem, sum_send, sum_recv, tok_send, tok_recv, red_send, red_recv, disp_send, disp_recv, ag_send, ag_recv, fw_send, fw_recv,
    pair_send, pair_recv, hop_send, hop_recv, line_send, line_recv, ret_send, ret_recv,
):
    ne = nx * nz
    nt = ny * CORES
    tok = tokens_ref.shape[0]
    feat = tokens_ref.shape[1]
    two = wg.shape[0]
    blk = 2 * cap
    chunk = nx * blk
    e = lax.axis_index("expert")
    t = lax.axis_index("tensor")
    x, z = e // nz, e % nz
    y, c = t // CORES, t % CORES
    sib = y * CORES + (1 - c)

    order = [nz - 1, 2, nz - 2, 4, 3, nz - 3, 1, 0] if nz == 8 else list(range(nz))
    local = order.index(0)

    def is_wide(j):
        return j == local

    def wrap(v, n):
        v = jnp.where(v >= n, v - n, v)
        return jnp.where(v < 0, v + n, v)

    def offset(j):
        if isinstance(j, int):
            return order[j]
        return sum(jnp.where(j == k, dz, 0) for k, dz in enumerate(order))

    def expert_peer(j, dx, sign):
        return wrap(x + sign * dx, nx) * nz + wrap(z + sign * offset(j), nz)

    def tensor_peer(dy, core):
        return wrap(y + dy, ny) * CORES + core

    barrier = pltpu.get_barrier_semaphore()

    weights = [
        pltpu.make_async_copy(hbm, vmem, w_sem.at[i])
        for i, (hbm, vmem) in enumerate(((wg_hbm, wg), (wu_hbm, wu), (wd_hbm, wd)))
    ]
    for copy in weights:
        copy.start()
    for k in range(1, nt):
        pl.semaphore_signal(barrier, inc=1, device_id=(e, wrap(t + k, nt)), device_id_type=MESH)
    for j in range(nz):
        for dx in range(nx):
            if j != local or dx:
                pl.semaphore_signal(barrier, inc=1, device_id=(expert_peer(j, dx, 1), t), device_id_type=MESH)

    eye = (
        lax.broadcasted_iota(jnp.int32, (tok, tok), 0) == lax.broadcasted_iota(jnp.int32, (tok, tok), 1)
    ).astype(F32)
    values = tokens_ref[...].astype(F32)
    column = jnp.sum(values * values, axis=1, keepdims=True)
    row = jnp.sum(eye * column, axis=0, keepdims=True)
    sums[0] = jnp.broadcast_to(row, (8, tok))
    pl.semaphore_wait(barrier, ne - 1 + nt - 1)

    def sum_copy(k):
        return pltpu.make_async_remote_copy(
            sums.at[0], sums.at[k], sum_send.at[k], sum_recv.at[k],
            device_id=(e, wrap(t + k, nt)), device_id_type=MESH,
        )

    for k in range(1, nt):
        sum_copy(k).start()

    routes_t, shares_t = routes_ref[...].astype(F32), shares_ref[...].astype(F32)
    ids = lax.broadcasted_iota(jnp.int32, (2 * ne, tok), 0)
    expert_id = (2 * expert_peer(ids // (2 * nx), ids // 2 % nx, 1) + ids % 2).astype(F32)
    named = jnp.zeros((2 * ne, tok), F32)
    weight = jnp.zeros((2 * ne, tok), F32)
    for k in range(routes_t.shape[0]):
        hit = (expert_id == routes_t[k : k + 1, :]).astype(F32)
        named = named + hit
        weight = weight + hit * shares_t[k : k + 1, :]
    earlier = (
        lax.broadcasted_iota(jnp.int32, (tok, tok), 0) < lax.broadcasted_iota(jnp.int32, (tok, tok), 1)
    ).astype(F32).astype(BF16)
    slot = lax.dot_general(
        named.astype(BF16), earlier, (((1,), (0,)), ((), ())), preferred_element_type=F32
    )
    slot = jnp.where(named > 0.0, slot, -1.0)
    slots[...] = slot
    slot_share[...] = weight

    square = row
    for k in range(1, nt):
        sum_copy(k).wait()
        square = square + sums[k, 0:1, :]
    factor = lax.rsqrt(square * (1.0 / full_feat) + 1e-06)
    factor = jnp.sum(eye * factor, axis=1, keepdims=True)
    lanes = gain_ref.shape[1]
    for q in range(feat // lanes):
        cols = slice(q * lanes, (q + 1) * lanes)
        gain = gain_ref[pl.ds(t * (feat // lanes) + q, 1), :]
        normed[y, :, cols] = (values[:, cols] * factor * gain).astype(BF16)

    def token_copy(dy, row):
        return pltpu.make_async_remote_copy(
            normed.at[row], normed.at[row], tok_send.at[dy], tok_recv.at[dy],
            device_id=(e, tensor_peer(dy, c)), device_id_type=MESH,
        )

    for dy in range(1, ny):
        token_copy(dy, y).start()

    def block(j, dx):
        return pl.ds(j * chunk + dx * blk, blk)

    def wide_block(dx):
        return pl.ds(dx * blk, blk)

    def wide_dispatch(j, dx):
        return pltpu.make_async_remote_copy(
            wide_out.at[:, wide_block(dx)], rows_in.at[c, :, block(j, dx)],
            disp_send.at[j, dx], disp_recv.at[j, dx],
            device_id=(expert_peer(j, dx, 1), t), device_id_type=MESH,
        )

    def wide_give_back(j, dx):
        return pltpu.make_async_remote_copy(
            part.at[c, :, block(j, dx)], wide_back.at[:, wide_block(dx)],
            ret_send.at[j, dx], ret_recv.at[j, dx],
            device_id=(expert_peer(j, dx, -1), t), device_id_type=MESH,
        )

    def dispatch(j, dx):
        return pltpu.make_async_remote_copy(
            outgoing.at[block(j, dx)], rows_in.at[c, y, block(j, dx)], disp_send.at[j, dx], disp_recv.at[j, dx],
            device_id=(expert_peer(j, dx, 1), t), device_id_type=MESH,
        )

    def give_back(j, dx):
        return pltpu.make_async_remote_copy(
            done.at[block(j, dx)], back.at[block(j, dx)], ret_send.at[j, dx], ret_recv.at[j, dx],
            device_id=(expert_peer(j, dx, -1), t), device_id_type=MESH,
        )

    def each(j, act):
        pl.when(j != local)(lambda: act(0))
        for dx in range(1, nx):
            act(dx)

    def stage_send(j):
        rows = whole(j)
        place = lax.broadcasted_iota(jnp.int32, (cap, tok), 0).astype(F32)
        for r in range(2 * nx):
            at = pl.ds(j * 2 * nx + r, 1)
            match = (slots[at, :] == place).astype(F32)
            pick[r * cap : (r + 1) * cap, :] = match
            share[pl.ds(j * chunk + r * cap, cap), :] = match * slot_share[at, :]
        chosen = pick[...].astype(BF16)

        @pl.when(jnp.logical_not(is_wide(j)))
        def _():
            outgoing[rows, :] = jnp.dot(chosen, normed[y], preferred_element_type=F32).astype(BF16)
            for dx in range(nx):
                dispatch(j, dx).start()

        @pl.when(j == local)
        def _():
            for dy in range(1, ny):
                token_copy(dy, wrap(y - dy, ny)).wait_recv()

        @pl.when(is_wide(j))
        def _():
            def slices(k, _):
                wide_out[k] = jnp.dot(
                    chosen, normed[k], preferred_element_type=F32
                ).astype(BF16)
                return 0

            lax.fori_loop(0, ny, slices, 0)
            each(j, lambda dx: wide_dispatch(j, dx).start())

        @pl.when(j == local)
        def _():
            for k in range(ny):
                rows_in[c, k, block(j, 0), :] = wide_out[k, wide_block(0), :]

    up, down = tensor_peer(1, c), tensor_peer(-1, c)
    half = chunk // 2

    def along(core, dy, rows, send, recv, target):
        ref = rows_in.at[core, wrap(y + dy, ny), rows]
        return pltpu.make_async_remote_copy(
            ref, ref, send, recv, device_id=(e, target), device_id_type=MESH,
        )

    def whole(j):
        return pl.ds(j * chunk, chunk)

    def piece(j, h):
        return pl.ds(j * chunk + h * half, half)

    def own_up(j, dy):
        return along(c, dy, whole(j), ag_send.at[j, 0], ag_recv.at[j, 0], up)

    def own_down(j, dy):
        return along(c, dy, whole(j), ag_send.at[j, 1], ag_recv.at[j, 1], down)

    def on_up(j, dy):
        return along(c, dy, piece(j, 0), ag_send.at[j, 2], ag_recv.at[j, 2], up)

    def on_down(j, dy):
        return along(c, dy, piece(j, 1), ag_send.at[j, 3], ag_recv.at[j, 3], down)

    def across(j, k, core, dy):
        return along(core, dy, whole(j), fw_send.at[j, k], fw_recv.at[j, k], sib)

    def wide_across(j, core):
        ref = rows_in.at[core, :, whole(j)]
        return pltpu.make_async_remote_copy(
            ref, ref, fw_send.at[j, 0], fw_recv.at[j, 0], device_id=(e, sib), device_id_type=MESH,
        )

    turns = (0, -1, 1, 2)

    def pair(j):
        rows = pl.ds(j * chunk, chunk)
        return pltpu.make_async_remote_copy(
            part.at[1 - c, :, rows], pair_in.at[:, rows], pair_send.at[j], pair_recv.at[j],
            device_id=(e, sib), device_id_type=MESH,
        )

    def hop(j, h):
        return pltpu.make_async_remote_copy(
            part.at[c, wrap(y + 2, ny), piece(j, h)], hop_in.at[h, pl.ds(j * half, half)],
            hop_send.at[j, h], hop_recv.at[j, h],
            device_id=(e, down if h else up), device_id_type=MESH,
        )

    def line(j, h):
        return pltpu.make_async_remote_copy(
            part.at[c, wrap(y + (-1 if h else 1), ny), whole(j)], line_in.at[h, whole(j)],
            line_send.at[j, h], line_recv.at[j, h],
            device_id=(e, down if h else up), device_id_type=MESH,
        )

    def stage_gather(j):
        @pl.when(is_wide(j))
        def _():
            each(j, lambda dx: wide_dispatch(j, dx).wait_recv())
            wide_across(j, c).start()

        @pl.when(jnp.logical_not(is_wide(j)))
        def _():
            for dx in range(nx):
                dispatch(j, dx).wait_recv()
            own_up(j, 0).start()
            own_down(j, 0).start()
            across(j, 0, c, 0).start()

    def stage_forward(j):
        @pl.when(jnp.logical_not(is_wide(j)))
        def _():
            own_up(j, -1).wait_recv()
            on_up(j, -1).start()
            across(j, 1, c, -1).start()
            own_down(j, 1).wait_recv()
            on_down(j, 1).start()
            across(j, 2, c, 1).start()

    def stage_far(j):
        @pl.when(jnp.logical_not(is_wide(j)))
        def _():
            on_up(j, 2).wait_recv()
            on_down(j, 2).wait_recv()
            across(j, 3, c, 2).start()

    def stage_expert(j):
        @pl.when(j == 0)
        def _():
            for copy in weights:
                copy.wait()

        @pl.when(is_wide(j))
        def _():
            wide_across(j, 1 - c).wait_recv()

        @pl.when(jnp.logical_not(is_wide(j)))
        def _():
            for k, dy in enumerate(turns):
                across(j, k, 1 - c, dy).wait_recv()

        rows = whole(j)
        acc[...] = jnp.zeros_like(acc)

        def widen(s, _):
            cols = pl.ds(pl.multiple_of(s * feat, feat), feat)
            lhs = rows_in[s % CORES, s // CORES, rows, :]
            nt_dims = (((1,), (1,)), ((), ()))
            acc[0] += lax.dot_general(lhs, wg[:, cols], nt_dims, preferred_element_type=F32)
            acc[1] += lax.dot_general(lhs, wu[:, cols], nt_dims, preferred_element_type=F32)
            return 0

        lax.fori_loop(0, nt, widen, 0)
        first_row = lax.broadcasted_iota(jnp.int32, (chunk, two), 0) % blk < cap
        first_col = lax.broadcasted_iota(jnp.int32, (chunk, two), 1) < two // 2
        gate = acc[0]
        hidden = gate * jax.nn.sigmoid(gate) * acc[1]
        hidden = jnp.where(first_row == first_col, hidden, 0.0).astype(BF16)

        def narrow(s, _):
            cols = pl.ds(pl.multiple_of(s * feat, feat), feat)
            part[s % CORES, s // CORES, rows, :] = jnp.dot(
                hidden, wd[:, cols], preferred_element_type=F32
            ).astype(BF16)
            return 0

        lax.fori_loop(0, nt, narrow, 0)
        pair(j).start()

    def stage_pair(j):
        rows = whole(j)
        pair(j).wait_recv()

        def join(dy):
            to = wrap(y + dy, ny)
            part[c, to, rows, :] = (
                part[c, to, rows, :].astype(F32) + pair_in[to, rows, :].astype(F32)
            ).astype(BF16)

        join(2)

        @pl.when(jnp.logical_not(is_wide(j)))
        def _():
            hop(j, 0).start()
            hop(j, 1).start()

        join(1)
        join(-1)

        @pl.when(is_wide(j))
        def _():
            join(0)
            each(j, lambda dx: wide_give_back(j, dx).start())

        @pl.when(j == local)
        def _():
            wide_back[:, wide_block(0), :] = part[c, :, block(j, 0), :]

    def stage_hop(j):
        @pl.when(jnp.logical_not(is_wide(j)))
        def _():
            for h in (0, 1):
                hop(j, h).wait_recv()
                to = wrap(y + (-1 if h else 1), ny)
                rows = piece(j, h)
                part[c, to, rows, :] = (
                    part[c, to, rows, :].astype(F32) + hop_in[h, pl.ds(j * half, half), :].astype(F32)
                ).astype(BF16)
                line(j, h).start()

    def stage_line(j):
        pl.when(jnp.logical_not(is_wide(j)))(lambda: finish(j))

    def finish(j):
        rows = whole(j)
        result = part[c, y, rows, :].astype(F32) + pair_in[y, rows, :].astype(F32)
        for h in (0, 1):
            line(j, h).wait_recv()
            result = result + line_in[h, rows, :].astype(F32)
        done[rows, :] = result.astype(BF16)

        for dx in range(nx):
            give_back(j, dx).start()

    def reduce(dy):
        return pltpu.make_async_remote_copy(
            red_out.at[dy - 1], red_in.at[dy - 1], red_send.at[dy - 1], red_recv.at[dy - 1],
            device_id=(e, tensor_peer(dy, c)), device_id_type=MESH,
        )

    def stage_mix(j):
        rows = whole(j)
        mine = share[rows, :].astype(BF16)
        onto = (((0,), (0,)), ((), ()))

        @pl.when(is_wide(j))
        def _():
            each(j, lambda dx: wide_give_back(j, dx).wait_recv())

            def slices(k, _):
                wide_total[k] += lax.dot_general(
                    mine, wide_back[k], onto, preferred_element_type=F32
                )
                return 0

            lax.fori_loop(0, ny, slices, 0)

        @pl.when(j == local)
        def _():
            for dy in (2, 1, ny - 1):
                red_out[dy - 1] = wide_total[wrap(y + dy, ny)].astype(BF16)
                reduce(dy).start()

        @pl.when(jnp.logical_not(is_wide(j)))
        def _():
            for dx in range(nx):
                give_back(j, dx).wait_recv()
            total[...] += lax.dot_general(mine, back[rows, :], onto, preferred_element_type=F32)

    def stage_drain(j):
        pair(j).wait_send()

        @pl.when(is_wide(j))
        def _():
            each(j, lambda dx: (wide_dispatch(j, dx).wait_send(), wide_give_back(j, dx).wait_send())[0])
            wide_across(j, c).wait_send()

        @pl.when(jnp.logical_not(is_wide(j)))
        def _():
            for dx in range(nx):
                dispatch(j, dx).wait_send()
                give_back(j, dx).wait_send()
            own_up(j, 0).wait_send()
            own_down(j, 0).wait_send()
            on_up(j, -1).wait_send()
            on_down(j, 1).wait_send()
            for k, dy in enumerate(turns):
                across(j, k, c, dy).wait_send()
            for h in (0, 1):
                hop(j, h).wait_send()
                line(j, h).wait_send()

    total[...] = jnp.zeros_like(total)
    wide_total[...] = jnp.zeros_like(wide_total)
    stages = (
        (0, stage_send), (2, stage_gather), (3, stage_forward), (4, stage_far), (5, stage_expert),
        (6, stage_pair), (7, stage_hop), (8, stage_line), (10, stage_mix), (10, stage_drain),
    )

    def step(i, _):
        for lag, stage in stages:
            @pl.when((i >= lag) & (i < nz + lag))
            def _(lag=lag, stage=stage):
                stage(i - lag)

        return 0

    lax.fori_loop(0, nz + stages[-1][0], step, 0)

    result = total[...] + wide_total[y]
    for dy in range(1, ny):
        token_copy(dy, y).wait_send()
        reduce(dy).wait()
        result = result + red_in[dy - 1].astype(F32)

    keep = (1.0 - skipped_ref[...].astype(F32)) / jnp.sum(shares_ref[...].astype(F32), axis=0, keepdims=True)
    keep = jnp.sum(eye * keep, axis=1, keepdims=True)
    out_ref[...] = (tokens_ref[...].astype(F32) + result * keep).astype(BF16)


def body(tokens, norm_gain, w_gate, w_up, w_down, routes, shares, skipped):
    ne = lax.axis_size("expert")
    nt = lax.axis_size("tensor")
    nz = LINE_Z
    nx = ne // nz
    ny = nt // CORES
    tok, feat = tokens.shape
    top = routes.shape[1]
    local, ff, full = w_gate.shape
    cap = tok * top * 3 // (2 * local * ne)
    rows = ne * local * cap
    chunk = nx * local * cap
    flat = [w.reshape(local * ff, full) for w in (w_gate, w_up, w_down)]
    vmem = pl.BlockSpec(memory_space=pltpu.VMEM)
    hbm = pl.BlockSpec(memory_space=pl.ANY)
    dma = pltpu.SemaphoreType.DMA
    return pl.pallas_call(
        functools.partial(kernel, nx, nz, ny, cap, full),
        out_shape=jax.ShapeDtypeStruct((tok, feat), BF16),
        in_specs=[vmem] * 5 + [hbm] * 3,
        out_specs=vmem,
        scratch_shapes=[
            pltpu.VMEM((local * ff, full), BF16),
            pltpu.VMEM((local * ff, full), BF16),
            pltpu.VMEM((local * ff, full), BF16),
            pltpu.VMEM((nt, 8, tok), F32),
            pltpu.VMEM((2 * ne, tok), F32),
            pltpu.VMEM((2 * ne, tok), F32),
            pltpu.VMEM((chunk, tok), F32),
            pltpu.VMEM((rows, tok), F32),
            pltpu.VMEM((ny, tok, feat), BF16),
            pltpu.VMEM((rows, feat), BF16),
            pltpu.VMEM((ny, chunk, feat), BF16),
            pltpu.VMEM((CORES, ny, rows, feat), BF16),
            pltpu.VMEM((2, chunk, local * ff), F32),
            pltpu.VMEM((CORES, ny, rows, feat), BF16),
            pltpu.VMEM((ny, rows, feat), BF16),
            pltpu.VMEM((2, rows // 2, feat), BF16),
            pltpu.VMEM((2, rows, feat), BF16),
            pltpu.VMEM((rows, feat), BF16),
            pltpu.VMEM((rows, feat), BF16),
            pltpu.VMEM((ny, chunk, feat), BF16),
            pltpu.VMEM((tok, feat), F32),
            pltpu.VMEM((ny, tok, feat), F32),
            pltpu.VMEM((ny - 1, tok, feat), BF16),
            pltpu.VMEM((ny - 1, tok, feat), BF16),
            dma((3,)),
            dma((nt,)),
            dma((nt,)),
            dma((ny,)),
            dma((ny,)),
            dma((ny - 1,)),
            dma((ny - 1,)),
            dma((nz, nx)),
            dma((nz, nx)),
            dma((nz, 4)),
            dma((nz, 4)),
            dma((nz, 4)),
            dma((nz, 4)),
            dma((nz,)),
            dma((nz,)),
            dma((nz, 2)),
            dma((nz, 2)),
            dma((nz, 2)),
            dma((nz, 2)),
            dma((nz, nx)),
            dma((nz, nx)),
        ],
        compiler_params=pltpu.CompilerParams(
            collective_id=0, has_side_effects=True, vmem_limit_bytes=60 * 2**20
        ),
    )(tokens, norm_gain.reshape(-1, 128), routes.T, shares.T, skipped.reshape(1, tok), *flat)


def solution(mesh):
    return jax.shard_map(
        body,
        mesh=mesh,
        in_specs=(
            P("expert", "tensor"),
            P(),
            P("expert", "tensor", None),
            P("expert", "tensor", None),
            P("expert", "tensor", None),
            P("expert", None),
            P("expert", None),
            P("expert"),
        ),
        out_specs=P("expert", "tensor"),
        check_vma=False,
    )
```

```python
import functools

import jax
import jax.numpy as jnp
from jax import lax
from jax.experimental import pallas as pl
from jax.experimental.pallas import tpu as pltpu
from jax.sharding import PartitionSpec as P

MESH = pl.DeviceIdType.MESH
LINE_Z = 8
CORES = 2
F32 = jnp.float32
BF16 = jnp.bfloat16


def kernel(
    nx, nz, ny, cap, full_feat,
    tokens_ref, gain_ref, routes_ref, shares_ref, skipped_ref, wg_hbm, wu_hbm, wd_hbm,
    out_ref,
    wg, wu, wd, sums, slots, slot_share, pick, share, normed, outgoing, wide_out, rows_in, acc, hidden, part, pair_in, hop_in, line_in, done, back, wide_back, total, wide_total, red_out, red_in,
    w_sem, sum_send, sum_recv, tok_send, tok_recv, red_send, red_recv, disp_send, disp_recv, ag_send, ag_recv, fw_send, fw_recv,
    pair_send, pair_recv, hop_send, hop_recv, line_send, line_recv, ret_send, ret_recv,
):
    ne = nx * nz
    nt = ny * CORES
    tok = tokens_ref.shape[0]
    feat = tokens_ref.shape[1]
    two = wg.shape[0]
    blk = 2 * cap
    chunk = nx * blk
    e = lax.axis_index("expert")
    t = lax.axis_index("tensor")
    x, z = e // nz, e % nz
    y, c = t // CORES, t % CORES
    sib = y * CORES + (1 - c)

    order = [nz - 1, 2, nz - 2, 4, 3, nz - 3, 0, 1] if nz == 8 else list(range(nz))
    local = order.index(0)

    def is_wide(j):
        return j == local

    def wrap(v, n):
        v = jnp.where(v >= n, v - n, v)
        return jnp.where(v < 0, v + n, v)

    def offset(j):
        if isinstance(j, int):
            return order[j]
        return sum(jnp.where(j == k, dz, 0) for k, dz in enumerate(order))

    def expert_peer(j, dx, sign):
        return wrap(x + sign * dx, nx) * nz + wrap(z + sign * offset(j), nz)

    def tensor_peer(dy, core):
        return wrap(y + dy, ny) * CORES + core

    barrier = pltpu.get_barrier_semaphore()

    weights = [
        pltpu.make_async_copy(hbm, vmem, w_sem.at[i])
        for i, (hbm, vmem) in enumerate(((wg_hbm, wg), (wu_hbm, wu), (wd_hbm, wd)))
    ]
    for copy in weights:
        copy.start()
    for k in range(1, nt):
        pl.semaphore_signal(barrier, inc=1, device_id=(e, wrap(t + k, nt)), device_id_type=MESH)
    for j in range(nz):
        for dx in range(nx):
            if j != local or dx:
                pl.semaphore_signal(barrier, inc=1, device_id=(expert_peer(j, dx, 1), t), device_id_type=MESH)

    eye = (
        lax.broadcasted_iota(jnp.int32, (tok, tok), 0) == lax.broadcasted_iota(jnp.int32, (tok, tok), 1)
    ).astype(F32)
    values = tokens_ref[...].astype(F32)
    column = jnp.sum(values * values, axis=1, keepdims=True)
    row = jnp.sum(eye * column, axis=0, keepdims=True)
    sums[0] = jnp.broadcast_to(row, (8, tok))
    pl.semaphore_wait(barrier, ne - 1 + nt - 1)

    def sum_copy(k):
        return pltpu.make_async_remote_copy(
            sums.at[0], sums.at[k], sum_send.at[k], sum_recv.at[k],
            device_id=(e, wrap(t + k, nt)), device_id_type=MESH,
        )

    for k in range(1, nt):
        sum_copy(k).start()

    routes_t, shares_t = routes_ref[...].astype(F32), shares_ref[...].astype(F32)
    ids = lax.broadcasted_iota(jnp.int32, (2 * ne, tok), 0)
    expert_id = (2 * expert_peer(ids // (2 * nx), ids // 2 % nx, 1) + ids % 2).astype(F32)
    named = jnp.zeros((2 * ne, tok), F32)
    weight = jnp.zeros((2 * ne, tok), F32)
    for k in range(routes_t.shape[0]):
        hit = (expert_id == routes_t[k : k + 1, :]).astype(F32)
        named = named + hit
        weight = weight + hit * shares_t[k : k + 1, :]
    earlier = (
        lax.broadcasted_iota(jnp.int32, (tok, tok), 0) < lax.broadcasted_iota(jnp.int32, (tok, tok), 1)
    ).astype(F32).astype(BF16)
    slot = lax.dot_general(
        named.astype(BF16), earlier, (((1,), (0,)), ((), ())), preferred_element_type=F32
    )
    slot = jnp.where(named > 0.0, slot, -1.0)
    slots[...] = slot
    slot_share[...] = weight

    square = row
    for k in range(1, nt):
        sum_copy(k).wait()
        square = square + sums[k, 0:1, :]
    factor = lax.rsqrt(square * (1.0 / full_feat) + 1e-06)
    factor = jnp.sum(eye * factor, axis=1, keepdims=True)
    lanes = gain_ref.shape[1]
    for q in range(feat // lanes):
        cols = slice(q * lanes, (q + 1) * lanes)
        gain = gain_ref[pl.ds(t * (feat // lanes) + q, 1), :]
        normed[y, :, cols] = (values[:, cols] * factor * gain).astype(BF16)

    def token_copy(dy, row):
        return pltpu.make_async_remote_copy(
            normed.at[row], normed.at[row], tok_send.at[dy], tok_recv.at[dy],
            device_id=(e, tensor_peer(dy, c)), device_id_type=MESH,
        )

    def block(j, dx):
        return pl.ds(j * chunk + dx * blk, blk)

    def wide_block(dx):
        return pl.ds(dx * blk, blk)

    def wide_dispatch(j, dx):
        return pltpu.make_async_remote_copy(
            wide_out.at[:, wide_block(dx)], rows_in.at[c, :, block(j, dx)],
            disp_send.at[j, dx], disp_recv.at[j, dx],
            device_id=(expert_peer(j, dx, 1), t), device_id_type=MESH,
        )

    def wide_give_back(j, dx):
        return pltpu.make_async_remote_copy(
            part.at[c, :, block(j, dx)], wide_back.at[:, wide_block(dx)],
            ret_send.at[j, dx], ret_recv.at[j, dx],
            device_id=(expert_peer(j, dx, -1), t), device_id_type=MESH,
        )

    def dispatch(j, dx):
        return pltpu.make_async_remote_copy(
            outgoing.at[block(j, dx)], rows_in.at[c, y, block(j, dx)], disp_send.at[j, dx], disp_recv.at[j, dx],
            device_id=(expert_peer(j, dx, 1), t), device_id_type=MESH,
        )

    def give_back(j, dx):
        return pltpu.make_async_remote_copy(
            done.at[block(j, dx)], back.at[block(j, dx)], ret_send.at[j, dx], ret_recv.at[j, dx],
            device_id=(expert_peer(j, dx, -1), t), device_id_type=MESH,
        )

    def each(j, act):
        pl.when(j != local)(lambda: act(0))
        for dx in range(1, nx):
            act(dx)

    def stage_send(j):
        rows = whole(j)
        place = lax.broadcasted_iota(jnp.int32, (cap, tok), 0).astype(F32)
        for r in range(2 * nx):
            at = pl.ds(j * 2 * nx + r, 1)
            match = (slots[at, :] == place).astype(F32)
            pick[r * cap : (r + 1) * cap, :] = match
            share[pl.ds(j * chunk + r * cap, cap), :] = match * slot_share[at, :]
        chosen = pick[...].astype(BF16)

        @pl.when(jnp.logical_not(is_wide(j)))
        def _():
            outgoing[rows, :] = jnp.dot(chosen, normed[y], preferred_element_type=F32).astype(BF16)
            for dx in range(nx):
                dispatch(j, dx).start()

        @pl.when(j == 1)
        def _():
            for dy in range(1, ny):
                token_copy(dy, y).start()

        @pl.when(j == local)
        def _():
            for dy in range(1, ny):
                token_copy(dy, wrap(y - dy, ny)).wait_recv()

        @pl.when(is_wide(j))
        def _():
            def slices(k, _):
                wide_out[k] = jnp.dot(
                    chosen, normed[k], preferred_element_type=F32
                ).astype(BF16)
                return 0

            lax.fori_loop(0, ny, slices, 0)
            each(j, lambda dx: wide_dispatch(j, dx).start())

        @pl.when(j == local)
        def _():
            for k in range(ny):
                rows_in[c, k, block(j, 0), :] = wide_out[k, wide_block(0), :]

    up, down = tensor_peer(1, c), tensor_peer(-1, c)
    half = chunk // 2

    def along(core, dy, rows, send, recv, target):
        ref = rows_in.at[core, wrap(y + dy, ny), rows]
        return pltpu.make_async_remote_copy(
            ref, ref, send, recv, device_id=(e, target), device_id_type=MESH,
        )

    def whole(j):
        return pl.ds(j * chunk, chunk)

    def piece(j, h):
        return pl.ds(j * chunk + h * half, half)

    def own_up(j, dy):
        return along(c, dy, whole(j), ag_send.at[j, 0], ag_recv.at[j, 0], up)

    def own_down(j, dy):
        return along(c, dy, whole(j), ag_send.at[j, 1], ag_recv.at[j, 1], down)

    def on_up(j, dy):
        return along(c, dy, piece(j, 0), ag_send.at[j, 2], ag_recv.at[j, 2], up)

    def on_down(j, dy):
        return along(c, dy, piece(j, 1), ag_send.at[j, 3], ag_recv.at[j, 3], down)

    def across(j, k, core, dy):
        return along(core, dy, whole(j), fw_send.at[j, k], fw_recv.at[j, k], sib)

    def wide_across(j, core):
        ref = rows_in.at[core, :, whole(j)]
        return pltpu.make_async_remote_copy(
            ref, ref, fw_send.at[j, 0], fw_recv.at[j, 0], device_id=(e, sib), device_id_type=MESH,
        )

    turns = (0, -1, 1, 2)

    def pair(j):
        rows = pl.ds(j * chunk, chunk)
        return pltpu.make_async_remote_copy(
            part.at[1 - c, :, rows], pair_in.at[:, rows], pair_send.at[j], pair_recv.at[j],
            device_id=(e, sib), device_id_type=MESH,
        )

    def hop(j, h):
        return pltpu.make_async_remote_copy(
            part.at[c, wrap(y + 2, ny), piece(j, h)], hop_in.at[h, pl.ds(j * half, half)],
            hop_send.at[j, h], hop_recv.at[j, h],
            device_id=(e, down if h else up), device_id_type=MESH,
        )

    def line(j, h):
        return pltpu.make_async_remote_copy(
            part.at[c, wrap(y + (-1 if h else 1), ny), whole(j)], line_in.at[h, whole(j)],
            line_send.at[j, h], line_recv.at[j, h],
            device_id=(e, down if h else up), device_id_type=MESH,
        )

    def stage_gather(j):
        @pl.when(is_wide(j))
        def _():
            each(j, lambda dx: wide_dispatch(j, dx).wait_recv())
            wide_across(j, c).start()

        @pl.when(jnp.logical_not(is_wide(j)))
        def _():
            for dx in range(nx):
                dispatch(j, dx).wait_recv()
            own_up(j, 0).start()
            own_down(j, 0).start()
            across(j, 0, c, 0).start()

    def stage_forward(j):
        @pl.when(jnp.logical_not(is_wide(j)))
        def _():
            own_up(j, -1).wait_recv()
            on_up(j, -1).start()
            across(j, 1, c, -1).start()
            own_down(j, 1).wait_recv()
            on_down(j, 1).start()
            across(j, 2, c, 1).start()

    def stage_far(j):
        @pl.when(jnp.logical_not(is_wide(j)))
        def _():
            on_up(j, 2).wait_recv()
            on_down(j, 2).wait_recv()
            across(j, 3, c, 2).start()

    def stage_expert(j):
        @pl.when(j == 0)
        def _():
            for copy in weights:
                copy.wait()

        @pl.when(is_wide(j))
        def _():
            wide_across(j, 1 - c).wait_recv()

        @pl.when(jnp.logical_not(is_wide(j)))
        def _():
            for k, dy in enumerate(turns):
                across(j, k, 1 - c, dy).wait_recv()

        rows = whole(j)
        acc[...] = jnp.zeros_like(acc)

        def widen(s, _):
            cols = pl.ds(pl.multiple_of(s * feat, feat), feat)
            lhs = rows_in[s % CORES, s // CORES, rows, :]
            nt_dims = (((1,), (1,)), ((), ()))
            acc[0] += lax.dot_general(lhs, wg[:, cols], nt_dims, preferred_element_type=F32)
            acc[1] += lax.dot_general(lhs, wu[:, cols], nt_dims, preferred_element_type=F32)
            return 0

        lax.fori_loop(0, nt, widen, 0)
        first_row = lax.broadcasted_iota(jnp.int32, (chunk, two), 0) % blk < cap
        first_col = lax.broadcasted_iota(jnp.int32, (chunk, two), 1) < two // 2
        gate = acc[0]
        mixed = gate * jax.nn.sigmoid(gate) * acc[1]
        hidden[...] = jnp.where(first_row == first_col, mixed, 0.0).astype(BF16)

    def stage_narrow(j):
        rows = whole(j)

        def narrow(s, _):
            cols = pl.ds(pl.multiple_of(s * feat, feat), feat)
            part[s % CORES, s // CORES, rows, :] = jnp.dot(
                hidden[...], wd[:, cols], preferred_element_type=F32
            ).astype(BF16)
            return 0

        lax.fori_loop(0, nt, narrow, 0)
        pair(j).start()

    def stage_pair(j):
        rows = whole(j)
        pair(j).wait_recv()

        def join(dy):
            to = wrap(y + dy, ny)
            part[c, to, rows, :] = (
                part[c, to, rows, :].astype(F32) + pair_in[to, rows, :].astype(F32)
            ).astype(BF16)

        join(2)

        @pl.when(jnp.logical_not(is_wide(j)))
        def _():
            hop(j, 0).start()
            hop(j, 1).start()

        join(1)
        join(-1)

        @pl.when(is_wide(j))
        def _():
            join(0)
            each(j, lambda dx: wide_give_back(j, dx).start())

        @pl.when(j == local)
        def _():
            wide_back[:, wide_block(0), :] = part[c, :, block(j, 0), :]

    def stage_hop(j):
        @pl.when(jnp.logical_not(is_wide(j)))
        def _():
            for h in (0, 1):
                hop(j, h).wait_recv()
                to = wrap(y + (-1 if h else 1), ny)
                rows = piece(j, h)
                part[c, to, rows, :] = (
                    part[c, to, rows, :].astype(F32) + hop_in[h, pl.ds(j * half, half), :].astype(F32)
                ).astype(BF16)
                line(j, h).start()

    def stage_line(j):
        pl.when(jnp.logical_not(is_wide(j)))(lambda: finish(j))

    def finish(j):
        rows = whole(j)
        result = part[c, y, rows, :].astype(F32) + pair_in[y, rows, :].astype(F32)
        for h in (0, 1):
            line(j, h).wait_recv()
            result = result + line_in[h, rows, :].astype(F32)
        done[rows, :] = result.astype(BF16)

        for dx in range(nx):
            give_back(j, dx).start()

    def reduce(dy):
        return pltpu.make_async_remote_copy(
            red_out.at[dy - 1], red_in.at[dy - 1], red_send.at[dy - 1], red_recv.at[dy - 1],
            device_id=(e, tensor_peer(dy, c)), device_id_type=MESH,
        )

    def stage_mix(j):
        rows = whole(j)
        mine = share[rows, :].astype(BF16)
        onto = (((0,), (0,)), ((), ()))

        @pl.when(is_wide(j))
        def _():
            each(j, lambda dx: wide_give_back(j, dx).wait_recv())

            def slices(k, _):
                wide_total[k] += lax.dot_general(
                    mine, wide_back[k], onto, preferred_element_type=F32
                )
                return 0

            lax.fori_loop(0, ny, slices, 0)

        @pl.when(j == local)
        def _():
            for dy in (2, 1, ny - 1):
                red_out[dy - 1] = wide_total[wrap(y + dy, ny)].astype(BF16)
                reduce(dy).start()

        @pl.when(jnp.logical_not(is_wide(j)))
        def _():
            for dx in range(nx):
                give_back(j, dx).wait_recv()
            total[...] += lax.dot_general(mine, back[rows, :], onto, preferred_element_type=F32)

    def stage_drain(j):
        pair(j).wait_send()

        @pl.when(is_wide(j))
        def _():
            each(j, lambda dx: (wide_dispatch(j, dx).wait_send(), wide_give_back(j, dx).wait_send())[0])
            wide_across(j, c).wait_send()

        @pl.when(jnp.logical_not(is_wide(j)))
        def _():
            for dx in range(nx):
                dispatch(j, dx).wait_send()
                give_back(j, dx).wait_send()
            own_up(j, 0).wait_send()
            own_down(j, 0).wait_send()
            on_up(j, -1).wait_send()
            on_down(j, 1).wait_send()
            for k, dy in enumerate(turns):
                across(j, k, c, dy).wait_send()
            for h in (0, 1):
                hop(j, h).wait_send()
                line(j, h).wait_send()

    total[...] = jnp.zeros_like(total)
    wide_total[...] = jnp.zeros_like(wide_total)
    stages = (
        (0, stage_send),
        (2, stage_gather),
        (3, stage_forward),
        (4, stage_far),
        (5, stage_expert),
        (7, stage_hop),
        (8, stage_line),
        (5, stage_narrow),
        (6, stage_pair),
        (10, stage_mix),
        (10, stage_drain),
    )

    def step(i, _):
        for lag, stage in stages:
            @pl.when((i >= lag) & (i < nz + lag))
            def _(lag=lag, stage=stage):
                stage(i - lag)

        return 0

    lax.fori_loop(0, nz + stages[-1][0], step, 0)

    result = total[...] + wide_total[y]
    for dy in range(1, ny):
        token_copy(dy, y).wait_send()
        reduce(dy).wait()
        result = result + red_in[dy - 1].astype(F32)

    keep = (1.0 - skipped_ref[...].astype(F32)) / jnp.sum(shares_ref[...].astype(F32), axis=0, keepdims=True)
    keep = jnp.sum(eye * keep, axis=1, keepdims=True)
    out_ref[...] = (tokens_ref[...].astype(F32) + result * keep).astype(BF16)


def body(tokens, norm_gain, w_gate, w_up, w_down, routes, shares, skipped):
    ne = lax.axis_size("expert")
    nt = lax.axis_size("tensor")
    nz = LINE_Z
    nx = ne // nz
    ny = nt // CORES
    tok, feat = tokens.shape
    top = routes.shape[1]
    local, ff, full = w_gate.shape
    cap = tok * top * 3 // (2 * local * ne)
    rows = ne * local * cap
    chunk = nx * local * cap
    flat = [w.reshape(local * ff, full) for w in (w_gate, w_up, w_down)]
    vmem = pl.BlockSpec(memory_space=pltpu.VMEM)
    hbm = pl.BlockSpec(memory_space=pl.ANY)
    dma = pltpu.SemaphoreType.DMA
    return pl.pallas_call(
        functools.partial(kernel, nx, nz, ny, cap, full),
        out_shape=jax.ShapeDtypeStruct((tok, feat), BF16),
        in_specs=[vmem] * 5 + [hbm] * 3,
        out_specs=vmem,
        scratch_shapes=[
            pltpu.VMEM((local * ff, full), BF16),
            pltpu.VMEM((local * ff, full), BF16),
            pltpu.VMEM((local * ff, full), BF16),
            pltpu.VMEM((nt, 8, tok), F32),
            pltpu.VMEM((2 * ne, tok), F32),
            pltpu.VMEM((2 * ne, tok), F32),
            pltpu.VMEM((chunk, tok), F32),
            pltpu.VMEM((rows, tok), F32),
            pltpu.VMEM((ny, tok, feat), BF16),
            pltpu.VMEM((rows, feat), BF16),
            pltpu.VMEM((ny, chunk, feat), BF16),
            pltpu.VMEM((CORES, ny, rows, feat), BF16),
            pltpu.VMEM((2, chunk, local * ff), F32),
            pltpu.VMEM((chunk, local * ff), BF16),
            pltpu.VMEM((CORES, ny, rows, feat), BF16),
            pltpu.VMEM((ny, rows, feat), BF16),
            pltpu.VMEM((2, rows // 2, feat), BF16),
            pltpu.VMEM((2, rows, feat), BF16),
            pltpu.VMEM((rows, feat), BF16),
            pltpu.VMEM((rows, feat), BF16),
            pltpu.VMEM((ny, chunk, feat), BF16),
            pltpu.VMEM((tok, feat), F32),
            pltpu.VMEM((ny, tok, feat), F32),
            pltpu.VMEM((ny - 1, tok, feat), BF16),
            pltpu.VMEM((ny - 1, tok, feat), BF16),
            dma((3,)),
            dma((nt,)),
            dma((nt,)),
            dma((ny,)),
            dma((ny,)),
            dma((ny - 1,)),
            dma((ny - 1,)),
            dma((nz, nx)),
            dma((nz, nx)),
            dma((nz, 4)),
            dma((nz, 4)),
            dma((nz, 4)),
            dma((nz, 4)),
            dma((nz,)),
            dma((nz,)),
            dma((nz, 2)),
            dma((nz, 2)),
            dma((nz, 2)),
            dma((nz, 2)),
            dma((nz, nx)),
            dma((nz, nx)),
        ],
        compiler_params=pltpu.CompilerParams(
            collective_id=0, has_side_effects=True, vmem_limit_bytes=60 * 2**20
        ),
    )(tokens, norm_gain.reshape(-1, 128), routes.T, shares.T, skipped.reshape(1, tok), *flat)


def solution(mesh):
    return jax.shard_map(
        body,
        mesh=mesh,
        in_specs=(
            P("expert", "tensor"),
            P(),
            P("expert", "tensor", None),
            P("expert", "tensor", None),
            P("expert", "tensor", None),
            P("expert", None),
            P("expert", None),
            P("expert"),
        ),
        out_specs=P("expert", "tensor"),
        check_vma=False,
    )
```
